128 devices in a mesh: row: 16 (over y, x_lo, core), col: 8 (over z, x_hi).
Axes of the slice: x: 4 (x_hi: 2, x_lo: 2; x = x_hi * 2 + x_lo), y: 4, z: 4, core: 2. Of those that a mesh axis runs over, the one named last changes fastest.
Arguments:
- dual_ops: float32 [16, 8, 2048, 2048], P('row', 'col'), as said below
- basis: float32 [16, 8, 4, 64, 512], P('row', 'col'), may hold values from -0.125 to 0.125
- coarse_inverse: float32 [8192, 8192], P('row', 'col')
- gap_rhs: float32 [16, 8, 4, 32, 512], P('row', 'col'), may hold values from -6 to 6
- coarse_rhs: float32 [16, 8, 32, 64], P('row', 'col'), may hold values from -6 to 6
- contact_mask: int32 [16, 8, 4, 512], P('row', 'col'), may hold values 0 or 1
Outputs:
- multipliers: float32 [16, 8, 4, 32, 512], P('row', 'col')
- projected_grad: float32 [16, 8, 4, 32, 512], P('row', 'col')
The draws below stay inside these ranges and needn't reach their ends.
Inputs may be any that keep to these rules, and one draw needn't show every extreme that they name: `dual_ops`: each subdomain's dual operator is symmetric and positive definite.
All inputs are finite; a program needn't handle non-finite values. No bound on the sum of `contact_mask` on one device may be relied on, other than what follows from the above.
Results may differ from the reference program's by a relative error of at most 0.00025.
Values sent between devices are 32-bit elements; how exact they have to be, the bound alone decides.
No kernel may reach another device: no remote copies, remote signals or barrier semaphores. Data moves between devices by JAX's collectives and lax.ppermute only.
A program may use at most 128 MiB of HBM per device.

```python
import math
import jax
import jax.numpy as jnp
from jax import lax

M = 2048
FACE = 512
K = 32
MDEV = 64
NMODES = 8192
ITERS = 6
N_ROW = 16
N_COL = 8


def draw_dual_ops(key, part):
    keys = jax.random.split(key, N_ROW * N_COL)
    limit = 4.0 / math.sqrt(M)

    def single(subkey):
        raw = jax.random.normal(subkey, (M, M), jnp.float32)
        offdiag = (raw + raw.T) * (0.5 / math.sqrt(M))
        offdiag = jnp.clip(offdiag, -limit, limit) * (1.0 - jnp.eye(M, dtype=jnp.float32))
        return offdiag + 2.5 * jnp.eye(M, dtype=jnp.float32)
    return lax.map(single, keys).reshape(N_ROW, N_COL, M, M)


def draw_coarse_inverse(key, part):
    raw = jax.random.normal(key, (NMODES, NMODES), jnp.float32)
    return jnp.eye(NMODES, dtype=jnp.float32) + raw * (0.3 / math.sqrt(NMODES))


def set_ends(values, own_key, low, high):
    place = [jax.random.randint(jax.random.fold_in(own_key, axis), (), 0, length) for axis, length in enumerate(values.shape)]
    widest = values.shape.index(max(values.shape))
    neighbour = place[:widest] + [(place[widest] + 1) % values.shape[widest]] + place[widest + 1:]
    return values.at[tuple(place)].set(low).at[tuple(neighbour)].set(high)


def level_of(stream_key, dims, cuts, low, top_value):
    def one(position, blocks):
        heights = jax.random.uniform(jax.random.fold_in(jax.random.fold_in(stream_key, 6), position), (blocks,), jnp.float32, low / len(cuts), top_value / len(cuts))
        return jnp.repeat(jnp.exp(heights), dims[position] // blocks).reshape((-1,) + (1,) * (len(dims) - position - 1))

    factor_of = one(*cuts[0])
    for cut in cuts[1:]:
        factor_of = factor_of * one(*cut)
    return factor_of


def noise(key, dims, spread, most, pieces=(), held_as=jnp.bfloat16):
    drawn = jax.random.normal(key, dims, jnp.float32) * spread
    if len(pieces) > 0:
        drawn = level_of(key, dims, pieces, -0.22, 0.18) * drawn
    return jnp.clip(drawn, min=-most, max=most).astype(held_as)


def setup_inputs(seed: int = 0) -> dict:
    splits = jax.random.split(jax.random.key(seed), 7)
    return {
        "dual_ops": draw_dual_ops(jax.random.fold_in(splits[6], 71), 0),
        "basis": noise(splits[1], (N_ROW, N_COL, 4, MDEV, FACE), M ** -0.5, 0.125, ((0, 16), (1, 8)), jnp.float32),
        "coarse_inverse": draw_coarse_inverse(jax.random.fold_in(splits[6], 71), 0),
        "gap_rhs": noise(splits[3], (N_ROW, N_COL, 4, K, FACE), 1.0, 6.0, ((0, 16), (1, 8)), jnp.float32),
        "coarse_rhs": noise(splits[4], (N_ROW, N_COL, K, MDEV), 1.0, 6.0, ((0, 16), (1, 8)), jnp.float32),
        "contact_mask": set_ends((jax.random.randint(splits[5], (N_ROW, N_COL, 4, FACE), 0, 2) < 1).astype(jnp.int32), jax.random.fold_in(splits[5], 1), 0, 1),
    }


HIGH = lax.Precision.HIGHEST


def neighbour_faces(values):
    zero_row = jnp.zeros_like(values[:1, :, 0])
    zero_col = jnp.zeros_like(values[:, :1, 0])
    from_above = jnp.concatenate([zero_row, values[:-1, :, 1]], axis=0)
    from_below = jnp.concatenate([values[1:, :, 0], zero_row], axis=0)
    from_left = jnp.concatenate([zero_col, values[:, :-1, 3]], axis=1)
    from_right = jnp.concatenate([values[:, 1:, 2], zero_col], axis=1)
    return jnp.stack([from_above, from_below, from_left, from_right], axis=2)


def interface_sum(values):
    return values + neighbour_faces(values)


def reference(dual_ops, basis, coarse_inverse, gap_rhs, coarse_rhs, contact_mask):
    blocks = dual_ops.reshape(N_ROW, N_COL, 4, FACE, 4, FACE)

    def apply_dual(vector):
        return jnp.einsum("rcgjfi,rcfki->rcgkj", blocks, vector, precision=HIGH)

    def expand(amps):
        return jnp.einsum("rcfji,rckj->rcfki", basis, amps, precision=HIGH)

    def restrict(vector):
        return jnp.einsum("rcfji,rcfki->rckj", basis, vector, precision=HIGH)

    def coarse(coef):
        column_major = jnp.transpose(coef, (2, 1, 0, 3)).reshape(K, NMODES)
        amps = jnp.dot(column_major, coarse_inverse.T, precision=HIGH, preferred_element_type=jnp.float32)
        return jnp.transpose(amps.reshape(K, N_ROW, N_COL, MDEV), (1, 2, 0, 3))

    row_ids = jnp.arange(N_ROW)[:, None]
    col_ids = jnp.arange(N_COL)[None, :]
    has_nb = jnp.stack([
        jnp.broadcast_to(row_ids > 0, (N_ROW, N_COL)),
        jnp.broadcast_to(row_ids < N_ROW - 1, (N_ROW, N_COL)),
        jnp.broadcast_to(col_ids > 0, (N_ROW, N_COL)),
        jnp.broadcast_to(col_ids < N_COL - 1, (N_ROW, N_COL))], axis=2)
    weight = jnp.where(has_nb, 0.5, 1.0).astype(jnp.float32)[:, :, :, None, None]
    contact = jnp.logical_and(contact_mask == 1, jnp.logical_not(has_nb)[:, :, :, None])[:, :, :, None, :]

    dvec = interface_sum(gap_rhs)
    multipliers = interface_sum(expand(coarse(coarse_rhs)))
    projected = jnp.zeros_like(multipliers)
    for step in range(ITERS):
        grad = interface_sum(apply_dual(multipliers)) - dvec
        projected = grad - interface_sum(expand(coarse(restrict(grad))))
        image = apply_dual(projected)
        numer = jnp.sum(weight * grad * projected, axis=(0, 1, 2, 4))
        denom = jnp.sum(projected * image, axis=(0, 1, 2, 4))
        ratio = numer / denom
        multipliers = multipliers - ratio[None, None, None, :, None] * projected
        multipliers = jnp.where(contact, jnp.maximum(multipliers, 0.0), multipliers)
    return multipliers, projected
```

```python
import functools

import jax
import jax.numpy as jnp
from jax import lax
from jax.experimental import pallas as pl
from jax.experimental.pallas import tpu as pltpu
from jax.sharding import PartitionSpec as P

MDEV = 64
ITERS = 6
K = 32
FACE = 512
M = 4 * FACE
VMEM_LIMIT = 20 << 20

F32 = jnp.float32
BF16 = jnp.bfloat16


def split(x):
    hi = x.astype(BF16)
    return hi, (x - hi.astype(F32)).astype(BF16)


def call(kernel, outs, *args, scratch=(), smem=()):
    specs = [
        pl.BlockSpec(memory_space=pltpu.SMEM if i in smem else pltpu.VMEM)
        for i in range(len(args))
    ]
    return pl.pallas_call(
        kernel,
        out_shape=[jax.ShapeDtypeStruct(shape, dtype) for shape, dtype in outs],
        in_specs=specs,
        out_specs=[pl.BlockSpec(memory_space=pltpu.VMEM)] * len(outs),
        scratch_shapes=[pltpu.VMEM(shape, dtype) for shape, dtype in scratch],
        compiler_params=pltpu.CompilerParams(vmem_limit_bytes=VMEM_LIMIT),
    )(*args)


def split_kernel(x_ref, hi_ref, lo_ref):
    hi_ref[...], lo_ref[...] = split(x_ref[...])


def split_operator(dual):
    rows = 256
    return pl.pallas_call(
        split_kernel,
        grid=(M // rows,),
        out_shape=[jax.ShapeDtypeStruct((M, M), BF16)] * 2,
        in_specs=[pl.BlockSpec((rows, M), lambda i: (i, 0))],
        out_specs=[pl.BlockSpec((rows, M), lambda i: (i, 0))] * 2,
        compiler_params=pltpu.CompilerParams(vmem_limit_bytes=VMEM_LIMIT),
    )(dual)


def split_t_kernel(x_ref, hi_ref, lo_ref):
    hi_ref[...], lo_ref[...] = split(x_ref[...].T)


def split_tile(tile):
    rows, cols = tile.shape
    step = 256
    return pl.pallas_call(
        split_t_kernel,
        grid=(cols // step,),
        out_shape=[jax.ShapeDtypeStruct((cols, rows), BF16)] * 2,
        in_specs=[pl.BlockSpec((rows, step), lambda i: (0, i))],
        out_specs=[pl.BlockSpec((step, rows), lambda i: (i, 0))] * 2,
        compiler_params=pltpu.CompilerParams(vmem_limit_bytes=VMEM_LIMIT),
    )(tile)


def weights_kernel(has_ref, basis_ref, gap_ref, n0, n1, n2, n3, exp_ref, res_ref, dvec_ref):
    for f, n_ref in enumerate((n0, n1, n2, n3)):
        own = basis_ref[f]
        there = has_ref[f] != 0
        nb = jnp.where(there, n_ref[0:MDEV, :], 0.0)
        both = jnp.concatenate([own, nb] if f < 2 else [nb, own], axis=0)
        hi, lo = split(both)
        exp_ref[f, 0:128, :] = hi
        exp_ref[f, 128:256, :] = lo
        hi, lo = split(own)
        pair = jnp.concatenate([hi.astype(F32), lo.astype(F32)], axis=0)
        res_ref[f * FACE : (f + 1) * FACE, :] = pair.T.astype(BF16)
        dvec_ref[f] = gap_ref[f] + jnp.where(there, n_ref[MDEV : MDEV + K, :], 0.0)


def low_lanes(shape):
    return lax.broadcasted_iota(jnp.int32, shape, len(shape) - 1) < MDEV


def expand_faces(amps_ref, exp_ref):
    total = amps_ref[0]
    for s in range(1, amps_ref.shape[0]):
        total = total + amps_ref[s]
    own_up, left_down, right = total[0:K], total[K : 2 * K], total[2 * K : 3 * K]
    low = low_lanes((K, 128))
    own_high = pltpu.roll(own_up, MDEV, 1)
    sides = (
        own_up,
        jnp.where(low, own_up, left_down),
        jnp.where(low, left_down, own_high),
        jnp.where(low, right, own_high),
    )
    out = []
    for f, side in enumerate(sides):
        hi, lo = split(side)
        lhs = jnp.concatenate(
            [jnp.concatenate([hi, hi], axis=1), jnp.concatenate([lo, lo], axis=1)], axis=0
        )
        res = jnp.dot(lhs, exp_ref[f], preferred_element_type=F32)
        out.append(res[0:K] + res[K : 2 * K])
    return out


def put(lhs, f, value):
    hi, lo = split(value)
    lhs[0:K, f * FACE : (f + 1) * FACE] = hi
    lhs[K : 2 * K, f * FACE : (f + 1) * FACE] = lo


def apply_face(lhs, hi_ref, lo_ref, f):
    cols = slice(f * FACE, (f + 1) * FACE)
    a = jnp.dot(lhs[...], hi_ref[:, cols], preferred_element_type=F32)
    b = jnp.dot(lhs[0:K, :], lo_ref[:, cols], preferred_element_type=F32)
    return a[0:K] + a[K : 2 * K] + b


def first_kernel(amps_ref, exp_ref, hi_ref, lo_ref, m_ref, a0, a1, a2, a3, lhs):
    for f, face in enumerate(expand_faces(amps_ref, exp_ref)):
        m_ref[f] = face
        put(lhs, f, face)
    for f, a_ref in enumerate((a0, a1, a2, a3)):
        a_ref[...] = apply_face(lhs, hi_ref, lo_ref, f)


def step_face(sums_ref, contact_ref, m_ref, p_ref):
    sums = jnp.sum(sums_ref[...], axis=0)
    quot = sums / pltpu.roll(sums, 128 - K, 1)
    rows = lax.broadcasted_iota(jnp.int32, (K, 128), 0)
    lanes = lax.broadcasted_iota(jnp.int32, (K, 128), 1)
    ratio = jnp.sum(jnp.where(rows == lanes, quot, 0.0), axis=1, keepdims=True)
    for f in range(4):
        new = m_ref[f] - ratio * p_ref[f]
        yield f, jnp.where(contact_ref[f : f + 1, :] != 0, jnp.maximum(new, 0.0), new)


def step_kernel(
    sums_ref, contact_ref, m_ref, p_ref, hi_ref, lo_ref, new_ref, a0, a1, a2, a3, lhs
):
    for f, new in step_face(sums_ref, contact_ref, m_ref, p_ref):
        new_ref[f] = new
        put(lhs, f, new)
    for f, a_ref in enumerate((a0, a1, a2, a3)):
        a_ref[...] = apply_face(lhs, hi_ref, lo_ref, f)


def last_kernel(sums_ref, contact_ref, m_ref, p_ref, new_ref):
    for f, new in step_face(sums_ref, contact_ref, m_ref, p_ref):
        new_ref[f] = new


def grad_kernel(
    has_ref, a0, a1, a2, a3, n0, n1, n2, n3, dvec_ref, res_ref, grad_ref, e_ref, lhs
):
    for f, (a_ref, n_ref) in enumerate(((a0, n0), (a1, n1), (a2, n2), (a3, n3))):
        nb = jnp.where(has_ref[f] != 0, n_ref[...], 0.0)
        grad = a_ref[...] + nb - dvec_ref[f]
        grad_ref[f] = grad
        put(lhs, f, grad)
    both = jnp.dot(lhs[...], res_ref[...], preferred_element_type=F32)
    both = both[0:K] + both[K : 2 * K]
    e = both + pltpu.roll(both, MDEV, 1)
    packed = jnp.where(low_lanes((K // 2, 128)), e[0 : K // 2], e[K // 2 : K])
    for s in range(e_ref.shape[0]):
        e_ref[s] = packed


def coarse_kernel(x_ref, uh, ul, oh, ol, dh, dl, out_ref, lhs):
    half = K // 2
    low = low_lanes((half, 128))
    for t in range(x_ref.shape[0] // 2):
        xa, xb = x_ref[2 * t], x_ref[2 * t + 1]
        cols = slice(t * 128, (t + 1) * 128)
        top = jnp.where(low, xa, pltpu.roll(xb, MDEV, 1))
        bottom = jnp.where(low, pltpu.roll(xa, MDEV, 1), xb)
        lhs[0:half, cols], lhs[K : K + half, cols] = split(top)
        lhs[half:K, cols], lhs[K + half : 2 * K, cols] = split(bottom)

    def product(h_ref, l_ref):
        a = jnp.dot(lhs[...], h_ref[...], preferred_element_type=F32)
        b = jnp.dot(lhs[0:K, :], l_ref[...], preferred_element_type=F32)
        full = a[0:K] + a[K : 2 * K] + b
        blocks = [full[:, q * 128 : (q + 1) * 128] for q in range(full.shape[1] // 128)]
        return blocks, [pltpu.roll(b, MDEV, 1) for b in blocks]

    up, up_r = product(uh, ul)
    own, own_r = product(oh, ol)
    down, down_r = product(dh, dl)
    low = low_lanes((K, 128))
    zero = jnp.zeros((K, 128), F32)
    n = len(own)
    for q in range(n):
        even, odd = 2 * q, 2 * q + 1
        out_ref[even, 0:K, :] = jnp.where(low, own[q], up_r[q])
        out_ref[even, K : 2 * K, :] = jnp.where(low, own_r[q - 1] if q > 0 else zero, down_r[q])
        out_ref[even, 2 * K : 3 * K, :] = own_r[q]
        out_ref[odd, 0:K, :] = jnp.where(low, own_r[q], up[q])
        out_ref[odd, K : 2 * K, :] = jnp.where(low, own[q], down[q])
        out_ref[odd, 2 * K : 3 * K, :] = own[q + 1] if q + 1 < n else zero


def image_kernel(has_ref, amps_ref, grad_ref, exp_ref, hi_ref, lo_ref, p_ref, s_ref, lhs):
    numer = jnp.zeros((K, 1), F32)
    for f, face in enumerate(expand_faces(amps_ref, exp_ref)):
        grad = grad_ref[f]
        p = grad - face
        p_ref[f] = p
        put(lhs, f, p)
        weight = jnp.where(has_ref[f] != 0, 0.5, 1.0)
        numer = numer + weight * jnp.sum(grad * p, axis=1, keepdims=True)
    denom = jnp.zeros((K, 1), F32)
    for f in range(4):
        image = apply_face(lhs, hi_ref, lo_ref, f)
        denom = denom + jnp.sum(p_ref[f] * image, axis=1, keepdims=True)
    rows = lax.broadcasted_iota(jnp.int32, (K, 128), 0)
    lanes = lax.broadcasted_iota(jnp.int32, (K, 128), 1)
    placed = jnp.where(rows == lanes, numer, 0.0) + jnp.where(rows + K == lanes, denom, 0.0)
    line = jnp.sum(placed, axis=0, keepdims=True)
    s_ref[...] = jnp.broadcast_to(line[None], s_ref.shape)


def exchange(faces):
    def ring(axis, step):
        n = lax.axis_size(axis)
        return [(i, (i + step) % n) for i in range(n)]

    return (
        lax.ppermute(faces[1], "row", ring("row", 1)),
        lax.ppermute(faces[0], "row", ring("row", -1)),
        lax.ppermute(faces[3], "col", ring("col", 1)),
        lax.ppermute(faces[2], "col", ring("col", -1)),
    )


def shards(dual_ops, basis, coarse_inverse, gap_rhs, coarse_rhs, contact_mask):
    n_rows, n_cols = lax.axis_size("row"), lax.axis_size("col")
    row, col = lax.axis_index("row"), lax.axis_index("col")
    has_nb = jnp.stack([row > 0, row < n_rows - 1, col > 0, col < n_cols - 1]).astype(jnp.int32)
    contact = jnp.where(has_nb[:, None] != 0, 0, (contact_mask[0, 0] == 1).astype(jnp.int32))

    vec = ((4, K, FACE), F32)
    face = ((K, FACE), F32)
    split_lhs = ((2 * K, M), BF16)

    rhs = coarse_rhs[0, 0]
    packed = jnp.concatenate([rhs[: K // 2], rhs[K // 2 :]], axis=1)
    sent = jnp.broadcast_to(packed[None], (n_rows, K // 2, 2 * MDEV))

    both = jnp.concatenate([basis[0, 0], gap_rhs[0, 0]], axis=1)
    nbs = exchange([both[f] for f in range(4)])
    ring = [(i, (i + 1) % n_rows) for i in range(n_rows)]
    up_tile = lax.ppermute(coarse_inverse, "row", ring)
    down_tile = lax.ppermute(coarse_inverse, "row", [(b, a) for a, b in ring])

    hi, lo = split_operator(dual_ops[0, 0])
    exp, res, dvec = call(
        weights_kernel,
        [((4, 256, FACE), BF16), ((M, 128), BF16), vec],
        has_nb, basis[0, 0], gap_rhs[0, 0], *nbs,
        smem=(0,),
    )
    tiles = [*split_tile(up_tile), *split_tile(coarse_inverse), *split_tile(down_tile)]

    def coarse(sent):
        got = lax.all_to_all(sent, "row", 0, 0, tiled=True)
        (parts,) = call(
            coarse_kernel,
            [((n_cols, 3 * K, 128), F32)],
            got, *tiles,
            scratch=[((2 * K, n_rows * MDEV), BF16)],
        )
        return lax.all_to_all(parts, "col", 0, 0, tiled=True)

    amps = coarse(sent)
    multipliers, *applied = call(
        first_kernel, [vec] + [face] * 4, amps, exp, hi, lo, scratch=[split_lhs]
    )
    for step in range(ITERS):
        nbs = exchange(applied)
        grad, sent = call(
            grad_kernel,
            [vec, ((n_rows, K // 2, 128), F32)],
            has_nb, *applied, *nbs, dvec, res,
            scratch=[split_lhs], smem=(0,),
        )
        amps = coarse(sent)
        projected, sums = call(
            image_kernel,
            [vec, ((n_rows * n_cols, 1, 128), F32)],
            has_nb, amps, grad, exp, hi, lo,
            scratch=[split_lhs], smem=(0,),
        )
        sums = lax.all_to_all(sums, ("row", "col"), 0, 0, tiled=True)
        if step + 1 < ITERS:
            multipliers, *applied = call(
                step_kernel, [vec] + [face] * 4, sums, contact, multipliers, projected, hi, lo,
                scratch=[split_lhs],
            )
        else:
            (multipliers,) = call(last_kernel, [vec], sums, contact, multipliers, projected)
    return (multipliers[None, None], projected[None, None])


def solution(mesh):
    return jax.shard_map(
        shards,
        mesh=mesh,
        in_specs=(
            P("row", "col", None, None),
            P("row", "col", None, None, None),
            P("row", "col"),
            P("row", "col", None, None, None),
            P("row", "col", None, None),
            P("row", "col", None, None),
        ),
        out_specs=(P("row", "col", None, None, None), P("row", "col", None, None, None)),
        check_vma=False,
    )
```

```python
import functools

import jax
import jax.numpy as jnp
from jax import lax
from jax.experimental import pallas as pl
from jax.experimental.pallas import tpu as pltpu
from jax.sharding import PartitionSpec as P

MDEV = 64
ITERS = 6
K = 32
FACE = 512
M = 4 * FACE
DEPTH = 256
VMEM_LIMIT = 24 << 20

F32 = jnp.float32
BF16 = jnp.bfloat16


def split(x):
    hi = x.astype(BF16)
    return hi, (x - hi.astype(F32)).astype(BF16)


def call(kernel, outs, *args, scratch=(), smem=()):
    return pl.pallas_call(
        kernel,
        out_shape=[jax.ShapeDtypeStruct(shape, dtype) for shape, dtype in outs],
        in_specs=[
            pl.BlockSpec(memory_space=pltpu.SMEM if i in smem else pltpu.VMEM)
            for i in range(len(args))
        ],
        out_specs=[pl.BlockSpec(memory_space=pltpu.VMEM)] * len(outs),
        scratch_shapes=[pltpu.VMEM(shape, dtype) for shape, dtype in scratch],
        compiler_params=pltpu.CompilerParams(vmem_limit_bytes=VMEM_LIMIT),
    )(*args)


def split_t_kernel(x_ref, hi_ref, lo_ref):
    hi_ref[...], lo_ref[...] = split(x_ref[...].T)


def split_tile(tile):
    rows, cols = tile.shape
    step = 256
    return pl.pallas_call(
        split_t_kernel,
        grid=(cols // step,),
        out_shape=[jax.ShapeDtypeStruct((cols, rows), BF16)] * 2,
        in_specs=[pl.BlockSpec((rows, step), lambda i: (0, i))],
        out_specs=[pl.BlockSpec((step, rows), lambda i: (i, 0))] * 2,
        compiler_params=pltpu.CompilerParams(vmem_limit_bytes=VMEM_LIMIT),
    )(tile)


def weights_kernel(
    has_ref, mask_ref, basis_ref, gap_ref, n0, n1, n2, n3, exp_ref, res_ref, dvec_ref, contact_ref
):
    for f, n_ref in enumerate((n0, n1, n2, n3)):
        own = basis_ref[f]
        there = has_ref[f] != 0
        nb = jnp.where(there, n_ref[0:MDEV, :], 0.0)
        both = jnp.concatenate([nb, own] if f == 2 else [own, nb], axis=0)
        hi, lo = split(both)
        exp_ref[f, 0:128, :] = hi
        exp_ref[f, 128:256, :] = lo
        hi, lo = split(own)
        pair = jnp.concatenate([hi.astype(F32), lo.astype(F32)], axis=0)
        res_ref[f * FACE : (f + 1) * FACE, :] = pair.T.astype(BF16)
        dvec_ref[f] = gap_ref[f] + jnp.where(there, n_ref[MDEV : MDEV + K, :], 0.0)
        touch = jnp.where(mask_ref[f : f + 1, :] == 1, 1, 0)
        contact_ref[f : f + 1, :] = jnp.where(there, 0, touch)


def low_lanes(shape):
    return lax.broadcasted_iota(jnp.int32, shape, len(shape) - 1) < MDEV


def put(lhs, f, value):
    hi, lo = split(value)
    lhs[0:K, f * FACE : (f + 1) * FACE] = hi
    lhs[K : 2 * K, f * FACE : (f + 1) * FACE] = lo


def expand_face(side, weights):
    hi, lo = split(side)
    lhs = jnp.concatenate(
        [jnp.concatenate([hi, hi], axis=1), jnp.concatenate([lo, lo], axis=1)], axis=0
    )
    res = jnp.dot(lhs, weights, preferred_element_type=F32)
    return res[0:K] + res[K : 2 * K]


def product(lhs, first, block):
    last = first + block.shape[0]
    hi, lo = split(block)
    a = jnp.dot(lhs[:, first:last], hi, preferred_element_type=F32)
    b = jnp.dot(lhs[0:K, first:last], lo, preferred_element_type=F32)
    return a[0:K] + a[K : 2 * K] + b


def apply_face(lhs, dual, f):
    cols = slice(f * FACE, (f + 1) * FACE)
    total = jnp.zeros((K, FACE), F32)
    for first in range(0, M, DEPTH):
        total = total + product(lhs, first, dual[first : first + DEPTH, cols])
    return total


def amps_sides(own, pair, up, down):
    low = low_lanes((K, 128))
    return (
        jnp.where(low, own, up),
        jnp.where(low, own, down),
        jnp.where(low, pair, own),
        jnp.where(low, own, pair),
    )


def amps_kernel(parts_ref, own_ref, pair_ref):
    half = K // 2
    total = parts_ref[0]
    for s in range(1, parts_ref.shape[0]):
        total = total + parts_ref[s]
    pair_ref[...] = total[0:K]
    packed = total[K : K + half]
    turned = pltpu.roll(packed, MDEV, 1)
    low = low_lanes((half, 128))
    own_ref[0:half, :] = jnp.where(low, packed, turned)
    own_ref[half:K, :] = jnp.where(low, turned, packed)


def first_kernel(
    own_ref, pair_ref, up_ref, down_ref, exp_ref, dual, m_ref, a0, a1, a2, a3, lhs
):
    sides = amps_sides(own_ref[...], pair_ref[...], up_ref[...], down_ref[...])
    for f, side in enumerate(sides):
        face = expand_face(side, exp_ref[f])
        m_ref[f] = face
        put(lhs, f, face)
    for f, a_ref in enumerate((a0, a1, a2, a3)):
        a_ref[...] = apply_face(lhs, dual, f)


def ratio_of(sums_ref):
    sums = jnp.sum(sums_ref[...], axis=0)
    quot = sums / pltpu.roll(sums, 128 - K, 1)
    rows = lax.broadcasted_iota(jnp.int32, (K, 128), 0)
    lanes = lax.broadcasted_iota(jnp.int32, (K, 128), 1)
    return jnp.sum(jnp.where(rows == lanes, quot, 0.0), axis=1, keepdims=True)


def step_kernel(
    has_ref, sums_ref, contact_ref, m_ref, p_ref, image_ref, o0, o1, o2, o3, dual,
    new_ref, a0, a1, a2, a3, lhs, corr,
):
    ratio = ratio_of(sums_ref)
    for f in range(4):
        plain = m_ref[f] - ratio * p_ref[f]
        new = jnp.where(contact_ref[f : f + 1, :] != 0, jnp.maximum(plain, 0.0), plain)
        new_ref[f] = new
        corr[f] = new - plain
    faces = ((o0, a0), (o1, a1), (o2, a2), (o3, a3))
    for f, (o_ref, a_ref) in enumerate(faces):
        a_ref[...] = o_ref[...] - ratio * image_ref[f]
    for face in range(4):

        @pl.when(has_ref[face] == 0)
        def _():
            hi, lo = split(corr[face])
            lhs[0:K, :] = hi
            lhs[K : 2 * K, :] = lo
            for f, (_, a_ref) in enumerate(faces):
                total = a_ref[...]
                for first in range(0, FACE, DEPTH):
                    row = face * FACE + first
                    cols = slice(f * FACE, (f + 1) * FACE)
                    total = total + product(lhs, first, dual[row : row + DEPTH, cols])
                a_ref[...] = total


def last_kernel(sums_ref, contact_ref, m_ref, p_ref, new_ref):
    ratio = ratio_of(sums_ref)
    for f in range(4):
        new = m_ref[f] - ratio * p_ref[f]
        new_ref[f] = jnp.where(contact_ref[f : f + 1, :] != 0, jnp.maximum(new, 0.0), new)


def grad_kernel(
    has_ref, a0, a1, a2, a3, n0, n1, n2, n3, dvec_ref, res_ref, grad_ref, e_ref, lhs
):
    for f, (a_ref, n_ref) in enumerate(((a0, n0), (a1, n1), (a2, n2), (a3, n3))):
        nb = jnp.where(has_ref[f] != 0, n_ref[...], 0.0)
        grad = a_ref[...] + nb - dvec_ref[f]
        grad_ref[f] = grad
        put(lhs, f, grad)
    both = jnp.dot(lhs[...], res_ref[...], preferred_element_type=F32)
    both = both[0:K] + both[K : 2 * K]
    e = both + pltpu.roll(both, MDEV, 1)
    packed = jnp.where(low_lanes((K // 2, 128)), e[0 : K // 2], e[K // 2 : K])
    for s in range(e_ref.shape[0]):
        e_ref[s] = packed


def unpack_residuals(x_ref, lhs):
    half = K // 2
    low = low_lanes((half, 128))
    for t in range(x_ref.shape[0] // 2):
        xa, xb = x_ref[2 * t], x_ref[2 * t + 1]
        cols = slice(t * 128, (t + 1) * 128)
        top = jnp.where(low, xa, pltpu.roll(xb, MDEV, 1))
        bottom = jnp.where(low, pltpu.roll(xa, MDEV, 1), xb)
        lhs[0:half, cols], lhs[K : K + half, cols] = split(top)
        lhs[half:K, cols], lhs[K + half : 2 * K, cols] = split(bottom)


def coarse_kernel(x_ref, hi_ref, lo_ref, out_ref, lhs):
    unpack_residuals(x_ref, lhs)
    a = jnp.dot(lhs[...], hi_ref[...], preferred_element_type=F32)
    b = jnp.dot(lhs[0:K, :], lo_ref[...], preferred_element_type=F32)
    full = a[0:K] + a[K : 2 * K] + b
    own = [full[:, q : q + 128] for q in range(0, full.shape[1], 128)]
    turned = [pltpu.roll(b, MDEV, 1) for b in own]
    half, n = K // 2, len(own)
    low = low_lanes((K, 128))
    low_half = low_lanes((half, 128))
    zero = jnp.zeros((K, 128), F32)
    for q in range(n):
        even, odd = 2 * q, 2 * q + 1
        out_ref[even, 0:K, :] = jnp.where(low, turned[q - 1] if q > 0 else zero, own[q])
        out_ref[even, K : K + half, :] = jnp.where(low_half, own[q][0:half], turned[q][half:K])
        out_ref[odd, 0:K, :] = jnp.where(low, own[q], turned[q + 1] if q + 1 < n else zero)
        out_ref[odd, K : K + half, :] = jnp.where(low_half, turned[q][0:half], own[q][half:K])


def image_kernel(
    has_ref, own_ref, pair_ref, up_ref, down_ref, grad_ref, exp_ref, dual, p_ref, image_ref, s_ref, lhs
):
    sides = amps_sides(own_ref[...], pair_ref[...], up_ref[...], down_ref[...])
    numer = jnp.zeros((K, 1), F32)
    for f, side in enumerate(sides):
        grad = grad_ref[f]
        p = grad - expand_face(side, exp_ref[f])
        p_ref[f] = p
        put(lhs, f, p)
        weight = jnp.where(has_ref[f] != 0, 0.5, 1.0)
        numer = numer + weight * jnp.sum(grad * p, axis=1, keepdims=True)
    denom = jnp.zeros((K, 1), F32)
    for f in range(4):
        image = apply_face(lhs, dual, f)
        image_ref[f] = image
        denom = denom + jnp.sum(p_ref[f] * image, axis=1, keepdims=True)
    rows = lax.broadcasted_iota(jnp.int32, (K, 128), 0)
    lanes = lax.broadcasted_iota(jnp.int32, (K, 128), 1)
    placed = jnp.where(rows == lanes, numer, 0.0) + jnp.where(rows + K == lanes, denom, 0.0)
    line = jnp.sum(placed, axis=0, keepdims=True)
    s_ref[...] = jnp.broadcast_to(line[None], s_ref.shape)


def along(value, axis, step):
    n = lax.axis_size(axis)
    return lax.ppermute(value, axis, [(i, (i + step) % n) for i in range(n)])


def exchange(faces):
    return (
        along(faces[1], "row", 1),
        along(faces[0], "row", -1),
        along(faces[3], "col", 1),
        along(faces[2], "col", -1),
    )


def shards(dual_ops, basis, coarse_inverse, gap_rhs, coarse_rhs, contact_mask):
    n_rows, n_cols = lax.axis_size("row"), lax.axis_size("col")
    row, col = lax.axis_index("row"), lax.axis_index("col")
    has_nb = jnp.stack([row > 0, row < n_rows - 1, col > 0, col < n_cols - 1]).astype(jnp.int32)
    dual = dual_ops[0, 0]

    vec = ((4, K, FACE), F32)
    face = ((K, FACE), F32)
    amps = ((K, 128), F32)
    split_lhs = ((2 * K, M), BF16)

    tile = split_tile(coarse_inverse)

    def coarse(sent):
        got = lax.all_to_all(sent, "row", 0, 0, tiled=True)
        (parts,) = call(
            coarse_kernel, [((n_cols, K + K // 2, 128), F32)], got, *tile,
            scratch=[((2 * K, n_rows * MDEV), BF16)],
        )
        parts = lax.all_to_all(parts, "col", 0, 0, tiled=True)
        own, pair = call(amps_kernel, [amps, amps], parts)
        return own, pair, along(own, "row", 1), along(own, "row", -1)

    rhs = coarse_rhs[0, 0]
    packed = jnp.concatenate([rhs[: K // 2], rhs[K // 2 :]], axis=1)
    sent = jnp.broadcast_to(packed[None], (n_rows, K // 2, 2 * MDEV))

    both = jnp.concatenate([basis[0, 0], gap_rhs[0, 0]], axis=1)
    nbs = exchange([both[f] for f in range(4)])
    exp, res, dvec, contact = call(
        weights_kernel,
        [((4, 256, FACE), BF16), ((M, 128), BF16), vec, ((4, FACE), jnp.int32)],
        has_nb, contact_mask[0, 0], basis[0, 0], gap_rhs[0, 0], *nbs,
        smem=(0,),
    )

    sides = coarse(sent)
    exp, res, dvec, contact, sides = lax.optimization_barrier((exp, res, dvec, contact, sides))
    multipliers, *faces = call(
        first_kernel, [vec] + [face] * 4, *sides, exp, dual, scratch=[split_lhs]
    )
    for step in range(ITERS):
        grad, sent = call(
            grad_kernel,
            [vec, ((n_rows, K // 2, 128), F32)],
            has_nb, *faces, *exchange(faces), dvec, res,
            scratch=[split_lhs], smem=(0,),
        )
        projected, image, sums = call(
            image_kernel,
            [vec, vec, ((n_rows * n_cols, 1, 128), F32)],
            has_nb, *coarse(sent), grad, exp, dual,
            scratch=[split_lhs], smem=(0,),
        )
        sums = lax.all_to_all(sums, ("row", "col"), 0, 0, tiled=True)
        if step + 1 < ITERS:
            multipliers, *faces = call(
                step_kernel, [vec] + [face] * 4,
                has_nb, sums, contact, multipliers, projected, image, *faces, dual,
                scratch=[((2 * K, FACE), BF16), vec], smem=(0,),
            )
        else:
            (multipliers,) = call(last_kernel, [vec], sums, contact, multipliers, projected)
    return (multipliers[None, None], projected[None, None])


def solution(mesh):
    return jax.shard_map(
        shards,
        mesh=mesh,
        in_specs=(
            P("row", "col", None, None),
            P("row", "col", None, None, None),
            P("row", "col"),
            P("row", "col", None, None, None),
            P("row", "col", None, None),
            P("row", "col", None, None),
        ),
        out_specs=(P("row", "col", None, None, None), P("row", "col", None, None, None)),
        check_vma=False,
    )
```

```python
import functools

import jax
import jax.numpy as jnp
from jax import lax
from jax.experimental import pallas as pl
from jax.experimental.pallas import tpu as pltpu
from jax.sharding import PartitionSpec as P

MDEV = 64
ITERS = 6
K = 32
FACE = 512
M = 4 * FACE
DEPTH = 256
VMEM_LIMIT = 24 << 20

F32 = jnp.float32
BF16 = jnp.bfloat16


def split(x):
    hi = x.astype(BF16)
    return hi, (x - hi.astype(F32)).astype(BF16)


def call(kernel, outs, *args, scratch=(), smem=(), cost=None):
    return pl.pallas_call(
        kernel,
        out_shape=[jax.ShapeDtypeStruct(shape, dtype) for shape, dtype in outs],
        in_specs=[
            pl.BlockSpec(memory_space=pltpu.SMEM if i in smem else pltpu.VMEM)
            for i in range(len(args))
        ],
        out_specs=[pl.BlockSpec(memory_space=pltpu.VMEM)] * len(outs),
        scratch_shapes=[pltpu.VMEM(shape, dtype) for shape, dtype in scratch],
        cost_estimate=cost and pl.CostEstimate(flops=0, bytes_accessed=cost, transcendentals=0),
        compiler_params=pltpu.CompilerParams(vmem_limit_bytes=VMEM_LIMIT),
    )(*args)


def split_t_kernel(x_ref, hi_ref, lo_ref):
    hi_ref[...], lo_ref[...] = split(x_ref[...].T)


def split_tile(tile):
    rows, cols = tile.shape
    step = 256
    return pl.pallas_call(
        split_t_kernel,
        grid=(cols // step,),
        out_shape=[jax.ShapeDtypeStruct((cols, rows), BF16)] * 2,
        in_specs=[pl.BlockSpec((rows, step), lambda i: (0, i))],
        out_specs=[pl.BlockSpec((step, rows), lambda i: (i, 0))] * 2,
        compiler_params=pltpu.CompilerParams(vmem_limit_bytes=VMEM_LIMIT),
    )(tile)


def weights_kernel(
    has_ref, o0, o1, o2, o3, n0, n1, n2, n3, exp_ref, res_ref, dvec_ref, contact_ref
):
    for f, (o_ref, n_ref) in enumerate(((o0, n0), (o1, n1), (o2, n2), (o3, n3))):
        own = o_ref[0:MDEV, :]
        there = has_ref[f] != 0
        nb = jnp.where(there, n_ref[0:MDEV, :], 0.0)
        both = jnp.concatenate([nb, own] if f == 2 else [own, nb], axis=0)
        hi, lo = split(both)
        exp_ref[f, 0:128, :] = hi
        exp_ref[f, 128:256, :] = lo
        hi, lo = split(own)
        pair = jnp.concatenate([hi.astype(F32), lo.astype(F32)], axis=0)
        res_ref[f * FACE : (f + 1) * FACE, :] = pair.T.astype(BF16)
        gap = slice(MDEV, MDEV + K)
        dvec_ref[f] = o_ref[gap, :] + jnp.where(there, n_ref[gap, :], 0.0)
        touch = jnp.where(o_ref[MDEV + K : MDEV + K + 1, :] == 1.0, 1, 0)
        contact_ref[f : f + 1, :] = jnp.where(there, 0, touch)


def low_lanes(shape):
    return lax.broadcasted_iota(jnp.int32, shape, len(shape) - 1) < MDEV


def put(lhs, f, value):
    hi, lo = split(value)
    lhs[0:K, f * FACE : (f + 1) * FACE] = hi
    lhs[K : 2 * K, f * FACE : (f + 1) * FACE] = lo


def expand_face(side, weights):
    hi, lo = split(side)
    lhs = jnp.concatenate(
        [jnp.concatenate([hi, hi], axis=1), jnp.concatenate([lo, lo], axis=1)], axis=0
    )
    res = jnp.dot(lhs, weights, preferred_element_type=F32)
    return res[0:K] + res[K : 2 * K]


def product(lhs, first, block):
    last = first + block.shape[0]
    hi, lo = split(block)
    a = jnp.dot(lhs[:, first:last], hi, preferred_element_type=F32)
    b = jnp.dot(lhs[0:K, first:last], lo, preferred_element_type=F32)
    return a[0:K] + a[K : 2 * K] + b


def apply_rows(lhs, dual, f, total, first):
    cols = slice(f * FACE, (f + 1) * FACE)
    for k in range(0, lhs.shape[1], DEPTH):
        total = total + product(lhs, k, dual[first + k : first + k + DEPTH, cols])
    return total


def amps_kernel(parts_ref, own_ref, pair_ref):
    half = K // 2
    total = parts_ref[0]
    for s in range(1, parts_ref.shape[0]):
        total = total + parts_ref[s]
    pair_ref[...] = total[0:K]
    packed = total[K : K + half]
    turned = pltpu.roll(packed, MDEV, 1)
    low = low_lanes((half, 128))
    own_ref[0:half, :] = jnp.where(low, packed, turned)
    own_ref[half:K, :] = jnp.where(low, turned, packed)


def col_half_kernel(own_ref, pair_ref, grad_ref, exp_ref, dual, p_ref, part_ref, lhs):
    low = low_lanes((K, 128))
    own, pair = own_ref[...], pair_ref[...]
    for f, side in ((2, jnp.where(low, pair, own)), (3, jnp.where(low, own, pair))):
        p = grad_ref[f] - expand_face(side, exp_ref[f])
        p_ref[f - 2] = p
        put(lhs, f - 2, p)
    for f in range(4):
        part_ref[f] = apply_rows(lhs, dual, f, jnp.zeros((K, FACE), F32), M // 2)


def row_half(own_ref, up_ref, down_ref, exp_ref):
    low = low_lanes((K, 128))
    for f, nb_ref in ((0, up_ref), (1, down_ref)):
        yield f, expand_face(jnp.where(low, own_ref[...], nb_ref[...]), exp_ref[f])


def first_kernel(
    own_ref, pair_ref, up_ref, down_ref, exp_ref, dual, m_ref, a0, a1, a2, a3, buf, lhs, sems
):
    rows = buf.shape[1]
    copies = [
        pltpu.make_async_copy(dual.at[n * rows : (n + 1) * rows, :], buf.at[n], sems.at[n])
        for n in range(buf.shape[0])
    ]
    for copy in copies:
        copy.start()
    low = low_lanes((K, 128))
    own, pair = own_ref[...], pair_ref[...]
    for f, face in row_half(own_ref, up_ref, down_ref, exp_ref):
        m_ref[f] = face
        put(lhs, f, face)
    for f, side in ((2, jnp.where(low, pair, own)), (3, jnp.where(low, own, pair))):
        face = expand_face(side, exp_ref[f])
        m_ref[f] = face
        put(lhs, f, face)
    for n, copy in enumerate(copies):
        copy.wait()
        for f, a_ref in enumerate((a0, a1, a2, a3)):
            part = product(lhs, n * rows, buf[n, :, f * FACE : (f + 1) * FACE])
            a_ref[...] = part if n == 0 else a_ref[...] + part


def ratio_of(sums_ref):
    sums = jnp.sum(sums_ref[...], axis=0)
    quot = sums / pltpu.roll(sums, 128 - K, 1)
    rows = lax.broadcasted_iota(jnp.int32, (K, 128), 0)
    lanes = lax.broadcasted_iota(jnp.int32, (K, 128), 1)
    return jnp.sum(jnp.where(rows == lanes, quot, 0.0), axis=1, keepdims=True)


def add_clamped(has_ref, corr_ref, lhs, dual, faces):
    for face in range(4):

        @pl.when(has_ref[face] == 0)
        def _():
            hi, lo = split(corr_ref[face])
            lhs[0:K, :] = hi
            lhs[K : 2 * K, :] = lo
            for f, a_ref in faces:
                a_ref[...] = apply_rows(lhs, dual, f, a_ref[...], face * FACE)


def step_kernel(
    has_ref, sums_ref, contact_ref, m_ref, p_ref, image_ref, o0, o1, o2, o3, dual,
    new_ref, a0, a1, a2, a3, lhs, corr,
):
    ratio = ratio_of(sums_ref)
    faces = ((o0, a0), (o1, a1), (o2, a2), (o3, a3))
    for f, (o_ref, a_ref) in enumerate(faces):
        plain = m_ref[f] - ratio * p_ref[f]
        new = jnp.where(contact_ref[f : f + 1, :] != 0, jnp.maximum(plain, 0.0), plain)
        new_ref[f] = new
        corr[f] = new - plain
        a_ref[...] = o_ref[...] - ratio * image_ref[f]
    add_clamped(has_ref, corr, lhs, dual, [(f, a_ref) for f, (_, a_ref) in enumerate(faces)])


def last_kernel(sums_ref, contact_ref, m_ref, p_ref, new_ref):
    ratio = ratio_of(sums_ref)
    for f in range(4):
        new = m_ref[f] - ratio * p_ref[f]
        new_ref[f] = jnp.where(contact_ref[f : f + 1, :] != 0, jnp.maximum(new, 0.0), new)


def grad_kernel(
    has_ref, a0, a1, a2, a3, n0, n1, n2, n3, dvec_ref, res_ref, grad_ref, e_ref, lhs
):
    for f, (a_ref, n_ref) in enumerate(((a0, n0), (a1, n1), (a2, n2), (a3, n3))):
        nb = jnp.where(has_ref[f] != 0, n_ref[...], 0.0)
        grad = a_ref[...] + nb - dvec_ref[f]
        grad_ref[f] = grad
        put(lhs, f, grad)
    both = jnp.dot(lhs[...], res_ref[...], preferred_element_type=F32)
    both = both[0:K] + both[K : 2 * K]
    e = both + pltpu.roll(both, MDEV, 1)
    packed = jnp.where(low_lanes((K // 2, 128)), e[0 : K // 2], e[K // 2 : K])
    for s in range(e_ref.shape[0]):
        e_ref[s] = packed


def unpack_residuals(x_ref, lhs):
    half = K // 2
    low = low_lanes((half, 128))
    for t in range(x_ref.shape[0] // 2):
        xa, xb = x_ref[2 * t], x_ref[2 * t + 1]
        cols = slice(t * 128, (t + 1) * 128)
        top = jnp.where(low, xa, pltpu.roll(xb, MDEV, 1))
        bottom = jnp.where(low, pltpu.roll(xa, MDEV, 1), xb)
        lhs[0:half, cols], lhs[K : K + half, cols] = split(top)
        lhs[half:K, cols], lhs[K + half : 2 * K, cols] = split(bottom)


def coarse_kernel(x_ref, hi_ref, lo_ref, out_ref, lhs):
    unpack_residuals(x_ref, lhs)
    a = jnp.dot(lhs[...], hi_ref[...], preferred_element_type=F32)
    b = jnp.dot(lhs[0:K, :], lo_ref[...], preferred_element_type=F32)
    full = a[0:K] + a[K : 2 * K] + b
    own = [full[:, q : q + 128] for q in range(0, full.shape[1], 128)]
    turned = [pltpu.roll(b, MDEV, 1) for b in own]
    half, n = K // 2, len(own)
    low = low_lanes((K, 128))
    low_half = low_lanes((half, 128))
    zero = jnp.zeros((K, 128), F32)
    for q in range(n):
        even, odd = 2 * q, 2 * q + 1
        out_ref[even, 0:K, :] = jnp.where(low, turned[q - 1] if q > 0 else zero, own[q])
        out_ref[even, K : K + half, :] = jnp.where(low_half, own[q][0:half], turned[q][half:K])
        out_ref[odd, 0:K, :] = jnp.where(low, own[q], turned[q + 1] if q + 1 < n else zero)
        out_ref[odd, K : K + half, :] = jnp.where(low_half, turned[q][0:half], own[q][half:K])


def image_kernel(
    has_ref, own_ref, up_ref, down_ref, grad_ref, half_ref, part_ref, exp_ref, dual,
    p_ref, image_ref, s_ref, lhs,
):
    for f, face in row_half(own_ref, up_ref, down_ref, exp_ref):
        p = grad_ref[f] - face
        p_ref[f] = p
        p_ref[f + 2] = half_ref[f]
        put(lhs, f, p)
    numer = jnp.zeros((K, 1), F32)
    denom = jnp.zeros((K, 1), F32)
    for f in range(4):
        weight = jnp.where(has_ref[f] != 0, 0.5, 1.0)
        numer = numer + weight * jnp.sum(grad_ref[f] * p_ref[f], axis=1, keepdims=True)
        image = apply_rows(lhs, dual, f, part_ref[f], 0)
        image_ref[f] = image
        denom = denom + jnp.sum(p_ref[f] * image, axis=1, keepdims=True)
    rows = lax.broadcasted_iota(jnp.int32, (K, 128), 0)
    lanes = lax.broadcasted_iota(jnp.int32, (K, 128), 1)
    placed = jnp.where(rows == lanes, numer, 0.0) + jnp.where(rows + K == lanes, denom, 0.0)
    line = jnp.sum(placed, axis=0, keepdims=True)
    s_ref[...] = jnp.broadcast_to(line[None], s_ref.shape)


def along(value, axis, step):
    n = lax.axis_size(axis)
    return lax.ppermute(value, axis, [(i, (i + step) % n) for i in range(n)])


def exchange(faces):
    right = along(faces[3], "col", 1)
    left = along(faces[2], "col", -1)
    return along(faces[1], "row", 1), along(faces[0], "row", -1), right, left


def shards(dual_ops, basis, coarse_inverse, gap_rhs, coarse_rhs, contact_mask):
    n_rows, n_cols = lax.axis_size("row"), lax.axis_size("col")
    row, col = lax.axis_index("row"), lax.axis_index("col")
    has_nb = jnp.stack([row > 0, row < n_rows - 1, col > 0, col < n_cols - 1]).astype(jnp.int32)
    dual = dual_ops[0, 0]

    vec = ((4, K, FACE), F32)
    face = ((K, FACE), F32)
    amps = ((K, 128), F32)
    half = ((2, K, FACE), F32)
    half_lhs = ((2 * K, M // 2), BF16)

    def gather(sent):
        return lax.all_to_all(sent, "row", 0, 0, tiled=True)

    def amplitudes(got):
        (parts,) = call(
            coarse_kernel, [((n_cols, K + K // 2, 128), F32)], got, *tile,
            scratch=[((2 * K, n_rows * MDEV), BF16)],
        )
        parts = lax.all_to_all(parts, "col", 0, 0, tiled=True)
        return call(amps_kernel, [amps, amps], parts)

    def sides(own):
        return along(own, "row", 1), along(own, "row", -1)

    def col_half(own, pair, grad):
        return call(
            col_half_kernel, [half, vec], own, pair, grad, exp, dual,
            scratch=[half_lhs], cost=8 << 20,
        )

    def first(*args):
        slabs = 16
        return pl.pallas_call(
            first_kernel,
            out_shape=[jax.ShapeDtypeStruct(*vec)] + [jax.ShapeDtypeStruct(*face)] * 4,
            in_specs=[pl.BlockSpec(memory_space=pltpu.VMEM)] * (len(args) - 1)
            + [pl.BlockSpec(memory_space=pltpu.HBM)],
            out_specs=[pl.BlockSpec(memory_space=pltpu.VMEM)] * 5,
            scratch_shapes=[
                pltpu.VMEM((slabs, M // slabs, M), F32),
                pltpu.VMEM((2 * K, M), BF16),
                pltpu.SemaphoreType.DMA((slabs,)),
            ],
            compiler_params=pltpu.CompilerParams(vmem_limit_bytes=VMEM_LIMIT),
        )(*args[:-1], pltpu.with_memory_space_constraint(args[-1], pltpu.HBM))

    rhs = coarse_rhs[0, 0]
    packed = jnp.concatenate([rhs[: K // 2], rhs[K // 2 :]], axis=1)
    got = gather(jnp.broadcast_to(packed[None], (n_rows, K // 2, 2 * MDEV)))
    tile = split_tile(coarse_inverse)
    mask = jnp.broadcast_to(contact_mask[0, 0, :, None, :].astype(F32), (4, 8, FACE))
    both = jnp.concatenate([basis[0, 0], gap_rhs[0, 0], mask], axis=1)
    both = [both[f] for f in range(4)]
    own, pair = amplitudes(got)

    nbs = exchange(both)
    exp, res, dvec, contact = call(
        weights_kernel,
        [((4, 256, FACE), BF16), ((M, 128), BF16), vec, ((4, FACE), jnp.int32)],
        has_nb, *both, *nbs,
        smem=(0,),
    )
    multipliers, *faces = first(own, pair, *sides(own), exp, dual)
    faces, res, dvec, contact = lax.optimization_barrier((faces, res, dvec, contact))
    for step in range(ITERS):
        grad, sent = call(
            grad_kernel,
            [vec, ((n_rows, K // 2, 128), F32)],
            has_nb, *faces, *exchange(faces), dvec, res,
            scratch=[((2 * K, M), BF16)], smem=(0,),
        )
        own, pair = amplitudes(gather(sent))
        projected, image, sums = call(
            image_kernel,
            [vec, vec, ((n_rows * n_cols, 1, 128), F32)],
            has_nb, own, *sides(own), grad, *col_half(own, pair, grad), exp, dual,
            scratch=[half_lhs], smem=(0,),
        )
        sums = lax.all_to_all(sums, ("row", "col"), 0, 0, tiled=True)
        if step + 1 < ITERS:
            multipliers, *faces = call(
                step_kernel, [vec] + [face] * 4,
                has_nb, sums, contact, multipliers, projected, image, *faces, dual,
                scratch=[((2 * K, FACE), BF16), vec], smem=(0,),
            )
        else:
            (multipliers,) = call(last_kernel, [vec], sums, contact, multipliers, projected)
    return (multipliers[None, None], projected[None, None])


def solution(mesh):
    return jax.shard_map(
        shards,
        mesh=mesh,
        in_specs=(
            P("row", "col", None, None),
            P("row", "col", None, None, None),
            P("row", "col"),
            P("row", "col", None, None, None),
            P("row", "col", None, None),
            P("row", "col", None, None),
        ),
        out_specs=(P("row", "col", None, None, None), P("row", "col", None, None, None)),
        check_vma=False,
    )
```

```python
import functools

import jax
import jax.numpy as jnp
from jax import lax
from jax.experimental import pallas as pl
from jax.experimental.pallas import tpu as pltpu
from jax.sharding import PartitionSpec as P

MDEV = 64
ITERS = 6
K = 32
FACE = 512
M = 4 * FACE
DEPTH = 256
VMEM_LIMIT = 24 << 20

F32 = jnp.float32
BF16 = jnp.bfloat16


def split(x):
    hi = x.astype(BF16)
    return hi, (x - hi.astype(F32)).astype(BF16)


def call(kernel, outs, *args, scratch=(), smem=(), cost=None):
    return pl.pallas_call(
        kernel,
        out_shape=[jax.ShapeDtypeStruct(shape, dtype) for shape, dtype in outs],
        in_specs=[
            pl.BlockSpec(memory_space=pltpu.SMEM if i in smem else pltpu.VMEM)
            for i in range(len(args))
        ],
        out_specs=[pl.BlockSpec(memory_space=pltpu.VMEM)] * len(outs),
        scratch_shapes=[pltpu.VMEM(shape, dtype) for shape, dtype in scratch],
        cost_estimate=cost and pl.CostEstimate(flops=0, bytes_accessed=cost, transcendentals=0),
        compiler_params=pltpu.CompilerParams(vmem_limit_bytes=VMEM_LIMIT),
    )(*args)


def split_t_kernel(x_ref, hi_ref, lo_ref):
    hi_ref[...], lo_ref[...] = split(x_ref[...].T)


def split_tile(tile):
    rows, cols = tile.shape
    step = 256
    return pl.pallas_call(
        split_t_kernel,
        grid=(cols // step,),
        out_shape=[jax.ShapeDtypeStruct((cols, rows), BF16)] * 2,
        in_specs=[pl.BlockSpec((rows, step), lambda i: (0, i))],
        out_specs=[pl.BlockSpec((step, rows), lambda i: (i, 0))] * 2,
        compiler_params=pltpu.CompilerParams(vmem_limit_bytes=VMEM_LIMIT),
    )(tile)


def weights_kernel(
    has_ref, o0, o1, o2, o3, n0, n1, n2, n3, exp_ref, res_ref, dvec_ref, contact_ref
):
    for f, (o_ref, n_ref) in enumerate(((o0, n0), (o1, n1), (o2, n2), (o3, n3))):
        own = o_ref[0:MDEV, :]
        there = has_ref[f] != 0
        nb = jnp.where(there, n_ref[0:MDEV, :], 0.0)
        both = jnp.concatenate([nb, own] if f == 2 else [own, nb], axis=0)
        hi, lo = split(both)
        exp_ref[f, 0:128, :] = hi
        exp_ref[f, 128:256, :] = lo
        hi, lo = split(own)
        pair = jnp.concatenate([hi.astype(F32), lo.astype(F32)], axis=0)
        res_ref[f * FACE : (f + 1) * FACE, :] = pair.T.astype(BF16)
        gap = slice(MDEV, MDEV + K)
        dvec_ref[f] = o_ref[gap, :] + jnp.where(there, n_ref[gap, :], 0.0)
        touch = jnp.where(o_ref[MDEV + K : MDEV + K + 1, :] == 1.0, 1, 0)
        contact_ref[f : f + 1, :] = jnp.where(there, 0, touch)


def low_lanes(shape):
    return lax.broadcasted_iota(jnp.int32, shape, len(shape) - 1) < MDEV


def put(lhs, f, value):
    hi, lo = split(value)
    lhs[0:K, f * FACE : (f + 1) * FACE] = hi
    lhs[K : 2 * K, f * FACE : (f + 1) * FACE] = lo


def expand_face(side, weights):
    hi, lo = split(side)
    lhs = jnp.concatenate(
        [jnp.concatenate([hi, hi], axis=1), jnp.concatenate([lo, lo], axis=1)], axis=0
    )
    res = jnp.dot(lhs, weights, preferred_element_type=F32)
    return res[0:K] + res[K : 2 * K]


def product(lhs, first, block):
    last = first + block.shape[0]
    hi, lo = split(block)
    a = jnp.dot(lhs[:, first:last], hi, preferred_element_type=F32)
    b = jnp.dot(lhs[0:K, first:last], lo, preferred_element_type=F32)
    return a[0:K] + a[K : 2 * K] + b


def apply_rows(lhs, dual, f, total, first):
    cols = slice(f * FACE, (f + 1) * FACE)
    for k in range(0, lhs.shape[1], DEPTH):
        total = total + product(lhs, k, dual[first + k : first + k + DEPTH, cols])
    return total


def amps_kernel(parts_ref, own_ref, pair_ref):
    half = K // 2
    total = parts_ref[0]
    for s in range(1, parts_ref.shape[0]):
        total = total + parts_ref[s]
    pair_ref[...] = total[0:K]
    packed = total[K : K + half]
    turned = pltpu.roll(packed, MDEV, 1)
    low = low_lanes((half, 128))
    own_ref[0:half, :] = jnp.where(low, packed, turned)
    own_ref[half:K, :] = jnp.where(low, turned, packed)


def col_half_kernel(own_ref, pair_ref, grad_ref, exp_ref, dual, p_ref, part_ref, lhs):
    low = low_lanes((K, 128))
    own, pair = own_ref[...], pair_ref[...]
    for f, side in ((2, jnp.where(low, pair, own)), (3, jnp.where(low, own, pair))):
        p = grad_ref[f] - expand_face(side, exp_ref[f])
        p_ref[f - 2] = p
        put(lhs, f - 2, p)
    for f in range(4):
        part_ref[f] = apply_rows(lhs, dual, f, jnp.zeros((K, FACE), F32), M // 2)


def row_half(own_ref, up_ref, down_ref, exp_ref):
    low = low_lanes((K, 128))
    for f, nb_ref in ((0, up_ref), (1, down_ref)):
        yield f, expand_face(jnp.where(low, own_ref[...], nb_ref[...]), exp_ref[f])


def first_kernel(
    own_ref, pair_ref, up_ref, down_ref, exp_ref, dual, m_ref, a0, a1, a2, a3, buf, lhs, sems
):
    rows = buf.shape[1]
    copies = [
        pltpu.make_async_copy(dual.at[n * rows : (n + 1) * rows, :], buf.at[n], sems.at[n])
        for n in range(buf.shape[0])
    ]
    for copy in copies:
        copy.start()
    low = low_lanes((K, 128))
    own, pair = own_ref[...], pair_ref[...]
    for f, face in row_half(own_ref, up_ref, down_ref, exp_ref):
        m_ref[f] = face
        put(lhs, f, face)
    for f, side in ((2, jnp.where(low, pair, own)), (3, jnp.where(low, own, pair))):
        face = expand_face(side, exp_ref[f])
        m_ref[f] = face
        put(lhs, f, face)
    for n, copy in enumerate(copies):
        copy.wait()
        for f, a_ref in enumerate((a0, a1, a2, a3)):
            part = product(lhs, n * rows, buf[n, :, f * FACE : (f + 1) * FACE])
            a_ref[...] = part if n == 0 else a_ref[...] + part


def ratio_of(sums_ref):
    sums = jnp.sum(sums_ref[...], axis=0)
    quot = sums / pltpu.roll(sums, 128 - K, 1)
    rows = lax.broadcasted_iota(jnp.int32, (K, 128), 0)
    lanes = lax.broadcasted_iota(jnp.int32, (K, 128), 1)
    return jnp.sum(jnp.where(rows == lanes, quot, 0.0), axis=1, keepdims=True)


def add_clamped(has_ref, corr_ref, lhs, dual, faces, shared):
    for face in range(4):

        @pl.when(has_ref[face] == 0)
        def _():
            hi, lo = split(corr_ref[face])
            lhs[0:K, :] = hi
            lhs[K : 2 * K, :] = lo
            for f, a_ref in enumerate(faces):

                @pl.when((has_ref[f] != 0) == shared)
                def _():
                    a_ref[...] = apply_rows(lhs, dual, f, a_ref[...], face * FACE)


def step_kernel(
    has_ref, sums_ref, contact_ref, m_ref, p_ref, image_ref, o0, o1, o2, o3, dual,
    new_ref, corr, a0, a1, a2, a3, lhs,
):
    ratio = ratio_of(sums_ref)
    faces = ((o0, a0), (o1, a1), (o2, a2), (o3, a3))
    for f, (o_ref, a_ref) in enumerate(faces):
        plain = m_ref[f] - ratio * p_ref[f]
        new = jnp.where(contact_ref[f : f + 1, :] != 0, jnp.maximum(plain, 0.0), plain)
        new_ref[f] = new
        corr[f] = new - plain
        a_ref[...] = o_ref[...] - ratio * image_ref[f]
    add_clamped(has_ref, corr, lhs, dual, (a0, a1, a2, a3), True)


def outer_kernel(has_ref, corr, o0, o1, o2, o3, dual, a0, a1, a2, a3, lhs):
    for o_ref, a_ref in ((o0, a0), (o1, a1), (o2, a2), (o3, a3)):
        a_ref[...] = o_ref[...]
    add_clamped(has_ref, corr, lhs, dual, (a0, a1, a2, a3), False)


def last_kernel(sums_ref, contact_ref, m_ref, p_ref, new_ref):
    ratio = ratio_of(sums_ref)
    for f in range(4):
        new = m_ref[f] - ratio * p_ref[f]
        new_ref[f] = jnp.where(contact_ref[f : f + 1, :] != 0, jnp.maximum(new, 0.0), new)


def grad_kernel(
    has_ref, a0, a1, a2, a3, n0, n1, n2, n3, dvec_ref, res_ref, grad_ref, e_ref, lhs
):
    for f, (a_ref, n_ref) in enumerate(((a0, n0), (a1, n1), (a2, n2), (a3, n3))):
        nb = jnp.where(has_ref[f] != 0, n_ref[...], 0.0)
        grad = a_ref[...] + nb - dvec_ref[f]
        grad_ref[f] = grad
        put(lhs, f, grad)
    both = jnp.dot(lhs[...], res_ref[...], preferred_element_type=F32)
    both = both[0:K] + both[K : 2 * K]
    e = both + pltpu.roll(both, MDEV, 1)
    packed = jnp.where(low_lanes((K // 2, 128)), e[0 : K // 2], e[K // 2 : K])
    for s in range(e_ref.shape[0]):
        e_ref[s] = packed


def unpack_residuals(x_ref, lhs):
    half = K // 2
    low = low_lanes((half, 128))
    for t in range(x_ref.shape[0] // 2):
        xa, xb = x_ref[2 * t], x_ref[2 * t + 1]
        cols = slice(t * 128, (t + 1) * 128)
        top = jnp.where(low, xa, pltpu.roll(xb, MDEV, 1))
        bottom = jnp.where(low, pltpu.roll(xa, MDEV, 1), xb)
        lhs[0:half, cols], lhs[K : K + half, cols] = split(top)
        lhs[half:K, cols], lhs[K + half : 2 * K, cols] = split(bottom)


def coarse_kernel(x_ref, hi_ref, lo_ref, out_ref, lhs):
    unpack_residuals(x_ref, lhs)
    a = jnp.dot(lhs[...], hi_ref[...], preferred_element_type=F32)
    b = jnp.dot(lhs[0:K, :], lo_ref[...], preferred_element_type=F32)
    full = a[0:K] + a[K : 2 * K] + b
    own = [full[:, q : q + 128] for q in range(0, full.shape[1], 128)]
    turned = [pltpu.roll(b, MDEV, 1) for b in own]
    half, n = K // 2, len(own)
    low = low_lanes((K, 128))
    low_half = low_lanes((half, 128))
    zero = jnp.zeros((K, 128), F32)
    for q in range(n):
        even, odd = 2 * q, 2 * q + 1
        out_ref[even, 0:K, :] = jnp.where(low, turned[q - 1] if q > 0 else zero, own[q])
        out_ref[even, K : K + half, :] = jnp.where(low_half, own[q][0:half], turned[q][half:K])
        out_ref[odd, 0:K, :] = jnp.where(low, own[q], turned[q + 1] if q + 1 < n else zero)
        out_ref[odd, K : K + half, :] = jnp.where(low_half, turned[q][0:half], own[q][half:K])


def image_kernel(
    has_ref, own_ref, up_ref, down_ref, grad_ref, half_ref, part_ref, exp_ref, dual,
    p_ref, image_ref, s_ref, lhs,
):
    for f, face in row_half(own_ref, up_ref, down_ref, exp_ref):
        p = grad_ref[f] - face
        p_ref[f] = p
        p_ref[f + 2] = half_ref[f]
        put(lhs, f, p)
    numer = jnp.zeros((K, 1), F32)
    denom = jnp.zeros((K, 1), F32)
    for f in range(4):
        weight = jnp.where(has_ref[f] != 0, 0.5, 1.0)
        numer = numer + weight * jnp.sum(grad_ref[f] * p_ref[f], axis=1, keepdims=True)
        image = apply_rows(lhs, dual, f, part_ref[f], 0)
        image_ref[f] = image
        denom = denom + jnp.sum(p_ref[f] * image, axis=1, keepdims=True)
    rows = lax.broadcasted_iota(jnp.int32, (K, 128), 0)
    lanes = lax.broadcasted_iota(jnp.int32, (K, 128), 1)
    placed = jnp.where(rows == lanes, numer, 0.0) + jnp.where(rows + K == lanes, denom, 0.0)
    line = jnp.sum(placed, axis=0, keepdims=True)
    s_ref[...] = jnp.broadcast_to(line[None], s_ref.shape)


def along(value, axis, step):
    n = lax.axis_size(axis)
    return lax.ppermute(value, axis, [(i, (i + step) % n) for i in range(n)])


def exchange(faces):
    right = along(faces[3], "col", 1)
    left = along(faces[2], "col", -1)
    return along(faces[1], "row", 1), along(faces[0], "row", -1), right, left


def shards(dual_ops, basis, coarse_inverse, gap_rhs, coarse_rhs, contact_mask):
    n_rows, n_cols = lax.axis_size("row"), lax.axis_size("col")
    row, col = lax.axis_index("row"), lax.axis_index("col")
    has_nb = jnp.stack([row > 0, row < n_rows - 1, col > 0, col < n_cols - 1]).astype(jnp.int32)
    dual = dual_ops[0, 0]

    vec = ((4, K, FACE), F32)
    face = ((K, FACE), F32)
    amps = ((K, 128), F32)
    half = ((2, K, FACE), F32)
    half_lhs = ((2 * K, M // 2), BF16)

    def gather(sent):
        return lax.all_to_all(sent, "row", 0, 0, tiled=True)

    def amplitudes(got):
        (parts,) = call(
            coarse_kernel, [((n_cols, K + K // 2, 128), F32)], got, *tile,
            scratch=[((2 * K, n_rows * MDEV), BF16)],
        )
        parts = lax.all_to_all(parts, "col", 0, 0, tiled=True)
        return call(amps_kernel, [amps, amps], parts)

    def sides(own):
        return along(own, "row", 1), along(own, "row", -1)

    def col_half(own, pair, grad):
        return call(
            col_half_kernel, [half, vec], own, pair, grad, exp, dual,
            scratch=[half_lhs], cost=8 << 20,
        )

    def first(*args):
        slabs = 16
        return pl.pallas_call(
            first_kernel,
            out_shape=[jax.ShapeDtypeStruct(*vec)] + [jax.ShapeDtypeStruct(*face)] * 4,
            in_specs=[pl.BlockSpec(memory_space=pltpu.VMEM)] * (len(args) - 1)
            + [pl.BlockSpec(memory_space=pltpu.HBM)],
            out_specs=[pl.BlockSpec(memory_space=pltpu.VMEM)] * 5,
            scratch_shapes=[
                pltpu.VMEM((slabs, M // slabs, M), F32),
                pltpu.VMEM((2 * K, M), BF16),
                pltpu.SemaphoreType.DMA((slabs,)),
            ],
            compiler_params=pltpu.CompilerParams(vmem_limit_bytes=VMEM_LIMIT),
        )(*args[:-1], pltpu.with_memory_space_constraint(args[-1], pltpu.HBM))

    rhs = coarse_rhs[0, 0]
    packed = jnp.concatenate([rhs[: K // 2], rhs[K // 2 :]], axis=1)
    got = gather(jnp.broadcast_to(packed[None], (n_rows, K // 2, 2 * MDEV)))
    tile = split_tile(coarse_inverse)
    mask = jnp.broadcast_to(contact_mask[0, 0, :, None, :].astype(F32), (4, 8, FACE))
    both = jnp.concatenate([basis[0, 0], gap_rhs[0, 0], mask], axis=1)
    both = [both[f] for f in range(4)]
    own, pair = amplitudes(got)

    nbs = exchange(both)
    exp, res, dvec, contact = call(
        weights_kernel,
        [((4, 256, FACE), BF16), ((M, 128), BF16), vec, ((4, FACE), jnp.int32)],
        has_nb, *both, *nbs,
        smem=(0,),
    )
    multipliers, *faces = first(own, pair, *sides(own), exp, dual)
    faces, res, dvec, contact = lax.optimization_barrier((faces, res, dvec, contact))
    nbs = exchange(faces)
    for step in range(ITERS):
        grad, sent = call(
            grad_kernel,
            [vec, ((n_rows, K // 2, 128), F32)],
            has_nb, *faces, *nbs, dvec, res,
            scratch=[((2 * K, M), BF16)], smem=(0,),
        )
        own, pair = amplitudes(gather(sent))
        projected, image, sums = call(
            image_kernel,
            [vec, vec, ((n_rows * n_cols, 1, 128), F32)],
            has_nb, own, *sides(own), grad, *col_half(own, pair, grad), exp, dual,
            scratch=[half_lhs], smem=(0,),
        )
        sums = lax.all_to_all(sums, ("row", "col"), 0, 0, tiled=True)
        if step + 1 < ITERS:
            multipliers, corr, *sent_faces = call(
                step_kernel, [vec, vec] + [face] * 4,
                has_nb, sums, contact, multipliers, projected, image, *faces, dual,
                scratch=[((2 * K, FACE), BF16)], smem=(0,),
            )
            nbs = exchange(sent_faces)
            faces = call(
                outer_kernel, [face] * 4, has_nb, corr, *sent_faces, dual,
                scratch=[((2 * K, FACE), BF16)], smem=(0,), cost=4 << 20,
            )
        else:
            (multipliers,) = call(last_kernel, [vec], sums, contact, multipliers, projected)
    return (multipliers[None, None], projected[None, None])


def solution(mesh):
    return jax.shard_map(
        shards,
        mesh=mesh,
        in_specs=(
            P("row", "col", None, None),
            P("row", "col", None, None, None),
            P("row", "col"),
            P("row", "col", None, None, None),
            P("row", "col", None, None),
            P("row", "col", None, None),
        ),
        out_specs=(P("row", "col", None, None, None), P("row", "col", None, None, None)),
        check_vma=False,
    )
```

```python
import functools

import jax
import jax.numpy as jnp
from jax import lax
from jax.experimental import pallas as pl
from jax.experimental.pallas import tpu as pltpu
from jax.sharding import PartitionSpec as P

MDEV = 64
ITERS = 6
K = 32
FACE = 512
M = 4 * FACE
DEPTH = 256
VMEM_LIMIT = 24 << 20

F32 = jnp.float32
BF16 = jnp.bfloat16


def split(x):
    hi = x.astype(BF16)
    return hi, (x - hi.astype(F32)).astype(BF16)


def call(kernel, outs, *args, scratch=(), smem=(), cost=None):
    return pl.pallas_call(
        kernel,
        out_shape=[jax.ShapeDtypeStruct(shape, dtype) for shape, dtype in outs],
        in_specs=[
            pl.BlockSpec(memory_space=pltpu.SMEM if i in smem else pltpu.VMEM)
            for i in range(len(args))
        ],
        out_specs=[pl.BlockSpec(memory_space=pltpu.VMEM)] * len(outs),
        scratch_shapes=[pltpu.VMEM(shape, dtype) for shape, dtype in scratch],
        cost_estimate=cost and pl.CostEstimate(flops=0, bytes_accessed=cost, transcendentals=0),
        compiler_params=pltpu.CompilerParams(vmem_limit_bytes=VMEM_LIMIT),
    )(*args)


def split_t_kernel(x_ref, hi_ref, lo_ref):
    hi_ref[...], lo_ref[...] = split(x_ref[...].T)


def split_tile(tile):
    rows, cols = tile.shape
    step = 256
    return pl.pallas_call(
        split_t_kernel,
        grid=(cols // step,),
        out_shape=[jax.ShapeDtypeStruct((cols, rows), BF16)] * 2,
        in_specs=[pl.BlockSpec((rows, step), lambda i: (0, i))],
        out_specs=[pl.BlockSpec((step, rows), lambda i: (i, 0))] * 2,
        compiler_params=pltpu.CompilerParams(vmem_limit_bytes=VMEM_LIMIT),
    )(tile)


def weights_kernel(
    has_ref, o0, o1, o2, o3, n0, n1, n2, n3, exp_ref, res_ref, dvec_ref, contact_ref
):
    for f, (o_ref, n_ref) in enumerate(((o0, n0), (o1, n1), (o2, n2), (o3, n3))):
        own = o_ref[0:MDEV, :]
        there = has_ref[f] != 0
        nb = jnp.where(there, n_ref[0:MDEV, :], 0.0)
        both = jnp.concatenate([nb, own] if f == 2 else [own, nb], axis=0)
        hi, lo = split(both)
        exp_ref[f, 0:128, :] = hi
        exp_ref[f, 128:256, :] = lo
        hi, lo = split(own)
        pair = jnp.concatenate([hi.astype(F32), lo.astype(F32)], axis=0)
        res_ref[f * FACE : (f + 1) * FACE, :] = pair.T.astype(BF16)
        gap = slice(MDEV, MDEV + K)
        dvec_ref[f] = o_ref[gap, :] + jnp.where(there, n_ref[gap, :], 0.0)
        touch = jnp.where(o_ref[MDEV + K : MDEV + K + 1, :] == 1.0, 1, 0)
        contact_ref[f : f + 1, :] = jnp.where(there, 0, touch)


def low_lanes(shape):
    return lax.broadcasted_iota(jnp.int32, shape, len(shape) - 1) < MDEV


def put(lhs, f, value):
    hi, lo = split(value)
    lhs[0:K, f * FACE : (f + 1) * FACE] = hi
    lhs[K : 2 * K, f * FACE : (f + 1) * FACE] = lo


def expand_face(side, weights):
    hi, lo = split(side)
    lhs = jnp.concatenate(
        [jnp.concatenate([hi, hi], axis=1), jnp.concatenate([lo, lo], axis=1)], axis=0
    )
    res = jnp.dot(lhs, weights, preferred_element_type=F32)
    return res[0:K] + res[K : 2 * K]


def product(lhs, first, block):
    last = first + block.shape[0]
    hi, lo = split(block)
    a = jnp.dot(lhs[:, first:last], hi, preferred_element_type=F32)
    b = jnp.dot(lhs[0:K, first:last], lo, preferred_element_type=F32)
    return a[0:K] + a[K : 2 * K] + b


def apply_rows(lhs, dual, f, total, first):
    cols = slice(f * FACE, (f + 1) * FACE)
    for k in range(0, lhs.shape[1], DEPTH):
        total = total + product(lhs, k, dual[first + k : first + k + DEPTH, cols])
    return total


def amps_kernel(parts_ref, own_ref, pair_ref):
    half = K // 2
    total = parts_ref[0]
    for s in range(1, parts_ref.shape[0]):
        total = total + parts_ref[s]
    pair_ref[...] = total[0:K]
    packed = total[K : K + half]
    turned = pltpu.roll(packed, MDEV, 1)
    low = low_lanes((half, 128))
    own_ref[0:half, :] = jnp.where(low, packed, turned)
    own_ref[half:K, :] = jnp.where(low, turned, packed)


def numer_terms(has_ref, f, grad, p):
    return jnp.where(has_ref[f] != 0, 0.5, 1.0) * grad * p


def col_half_kernel(
    has_ref, own_ref, pair_ref, grad_ref, exp_ref, dual, p_ref, part_ref, numer_ref, lhs
):
    low = low_lanes((K, 128))
    own, pair = own_ref[...], pair_ref[...]
    for f, side in ((2, jnp.where(low, pair, own)), (3, jnp.where(low, own, pair))):
        p = grad_ref[f] - expand_face(side, exp_ref[f])
        p_ref[f - 2] = p
        put(lhs, f - 2, p)
        terms = numer_terms(has_ref, f, grad_ref[f], p)
        numer_ref[...] = terms if f == 2 else numer_ref[...] + terms
    for f in range(4):
        part_ref[f] = apply_rows(lhs, dual, f, jnp.zeros((K, FACE), F32), M // 2)


def row_half(own_ref, up_ref, down_ref, exp_ref):
    low = low_lanes((K, 128))
    for f, nb_ref in ((0, up_ref), (1, down_ref)):
        yield f, expand_face(jnp.where(low, own_ref[...], nb_ref[...]), exp_ref[f])


def first_kernel(
    own_ref, pair_ref, up_ref, down_ref, exp_ref, dual, m_ref, a0, a1, a2, a3, buf, lhs, sems
):
    rows = buf.shape[1]
    copies = [
        pltpu.make_async_copy(dual.at[n * rows : (n + 1) * rows, :], buf.at[n], sems.at[n])
        for n in range(buf.shape[0])
    ]
    for copy in copies:
        copy.start()
    low = low_lanes((K, 128))
    own, pair = own_ref[...], pair_ref[...]
    for f, face in row_half(own_ref, up_ref, down_ref, exp_ref):
        m_ref[f] = face
        put(lhs, f, face)
    for f, side in ((2, jnp.where(low, pair, own)), (3, jnp.where(low, own, pair))):
        face = expand_face(side, exp_ref[f])
        m_ref[f] = face
        put(lhs, f, face)
    for n, copy in enumerate(copies):
        copy.wait()
        for f, a_ref in enumerate((a0, a1, a2, a3)):
            part = product(lhs, n * rows, buf[n, :, f * FACE : (f + 1) * FACE])
            a_ref[...] = part if n == 0 else a_ref[...] + part


def ratio_of(sums_ref):
    sums = jnp.sum(sums_ref[...], axis=0)
    quot = sums / pltpu.roll(sums, 128 - K, 1)
    rows = lax.broadcasted_iota(jnp.int32, (K, 128), 0)
    lanes = lax.broadcasted_iota(jnp.int32, (K, 128), 1)
    return jnp.sum(jnp.where(rows == lanes, quot, 0.0), axis=1, keepdims=True)


def add_clamped(has_ref, corr_ref, lhs, dual, faces, shared):
    for face in range(4):

        @pl.when(has_ref[face] == 0)
        def _():
            hi, lo = split(corr_ref[face])
            lhs[0:K, :] = hi
            lhs[K : 2 * K, :] = lo
            for f, a_ref in enumerate(faces):

                @pl.when((has_ref[f] != 0) == shared)
                def _():
                    a_ref[...] = apply_rows(lhs, dual, f, a_ref[...], face * FACE)


def clamped(contact_ref, f, plain):
    return jnp.where(contact_ref[f : f + 1, :] != 0, jnp.maximum(plain, 0.0), plain)


def step_kernel(
    has_ref, sums_ref, contact_ref, m_ref, p_ref, image_ref, o0, o1, o2, o3, dual,
    ratio_ref, corr, a0, a1, a2, a3, lhs,
):
    ratio = ratio_of(sums_ref)
    ratio_ref[...] = jnp.broadcast_to(ratio, ratio_ref.shape)
    for f, (o_ref, a_ref) in enumerate(((o0, a0), (o1, a1), (o2, a2), (o3, a3))):
        a_ref[...] = o_ref[...] - ratio * image_ref[f]

        @pl.when(has_ref[f] == 0)
        def _():
            plain = m_ref[f] - ratio * p_ref[f]
            corr[f] = clamped(contact_ref, f, plain) - plain

    add_clamped(has_ref, corr, lhs, dual, (a0, a1, a2, a3), True)


def outer_kernel(
    has_ref, ratio_ref, contact_ref, m_ref, p_ref, corr, o0, o1, o2, o3, dual,
    new_ref, a0, a1, a2, a3, lhs,
):
    ratio = ratio_ref[:, 0:1]
    for f, (o_ref, a_ref) in enumerate(((o0, a0), (o1, a1), (o2, a2), (o3, a3))):
        a_ref[...] = o_ref[...]
        new_ref[f] = clamped(contact_ref, f, m_ref[f] - ratio * p_ref[f])
    add_clamped(has_ref, corr, lhs, dual, (a0, a1, a2, a3), False)


def last_kernel(sums_ref, contact_ref, m_ref, p_ref, new_ref):
    ratio = ratio_of(sums_ref)
    for f in range(4):
        new = m_ref[f] - ratio * p_ref[f]
        new_ref[f] = jnp.where(contact_ref[f : f + 1, :] != 0, jnp.maximum(new, 0.0), new)


def grad_kernel(
    has_ref, a0, a1, a2, a3, n0, n1, n2, n3, dvec_ref, res_ref, grad_ref, e_ref, lhs
):
    for f, (a_ref, n_ref) in enumerate(((a0, n0), (a1, n1), (a2, n2), (a3, n3))):
        nb = jnp.where(has_ref[f] != 0, n_ref[...], 0.0)
        grad = a_ref[...] + nb - dvec_ref[f]
        grad_ref[f] = grad
        put(lhs, f, grad)
    both = jnp.dot(lhs[...], res_ref[...], preferred_element_type=F32)
    both = both[0:K] + both[K : 2 * K]
    e = both + pltpu.roll(both, MDEV, 1)
    packed = jnp.where(low_lanes((K // 2, 128)), e[0 : K // 2], e[K // 2 : K])
    for s in range(e_ref.shape[0]):
        e_ref[s] = packed


def unpack_residuals(x_ref, lhs):
    half = K // 2
    low = low_lanes((half, 128))
    for t in range(x_ref.shape[0] // 2):
        xa, xb = x_ref[2 * t], x_ref[2 * t + 1]
        cols = slice(t * 128, (t + 1) * 128)
        top = jnp.where(low, xa, pltpu.roll(xb, MDEV, 1))
        bottom = jnp.where(low, pltpu.roll(xa, MDEV, 1), xb)
        lhs[0:half, cols], lhs[K : K + half, cols] = split(top)
        lhs[half:K, cols], lhs[K + half : 2 * K, cols] = split(bottom)


def coarse_kernel(x_ref, hi_ref, lo_ref, out_ref, lhs):
    unpack_residuals(x_ref, lhs)
    a = jnp.dot(lhs[...], hi_ref[...], preferred_element_type=F32)
    b = jnp.dot(lhs[0:K, :], lo_ref[...], preferred_element_type=F32)
    full = a[0:K] + a[K : 2 * K] + b
    own = [full[:, q : q + 128] for q in range(0, full.shape[1], 128)]
    turned = [pltpu.roll(b, MDEV, 1) for b in own]
    half, n = K // 2, len(own)
    low = low_lanes((K, 128))
    low_half = low_lanes((half, 128))
    zero = jnp.zeros((K, 128), F32)
    for q in range(n):
        even, odd = 2 * q, 2 * q + 1
        out_ref[even, 0:K, :] = jnp.where(low, turned[q - 1] if q > 0 else zero, own[q])
        out_ref[even, K : K + half, :] = jnp.where(low_half, own[q][0:half], turned[q][half:K])
        out_ref[odd, 0:K, :] = jnp.where(low, own[q], turned[q + 1] if q + 1 < n else zero)
        out_ref[odd, K : K + half, :] = jnp.where(low_half, turned[q][0:half], own[q][half:K])


def image_kernel(
    has_ref, own_ref, up_ref, down_ref, grad_ref, half_ref, part_ref, numer_ref,
    exp_ref, dual, p_ref, image_ref, s_ref, lhs,
):
    for f, face in row_half(own_ref, up_ref, down_ref, exp_ref):
        p = grad_ref[f] - face
        p_ref[f] = p
        p_ref[f + 2] = half_ref[f]
        put(lhs, f, p)
    numer = numer_ref[...]
    for f in range(2):
        numer = numer + numer_terms(has_ref, f, grad_ref[f], p_ref[f])
    numer = jnp.sum(numer, axis=1, keepdims=True)
    denom = jnp.zeros((K, FACE), F32)
    for f in range(4):
        image = apply_rows(lhs, dual, f, part_ref[f], 0)
        image_ref[f] = image
        denom = denom + p_ref[f] * image
    denom = jnp.sum(denom, axis=1, keepdims=True)
    rows = lax.broadcasted_iota(jnp.int32, (K, 128), 0)
    lanes = lax.broadcasted_iota(jnp.int32, (K, 128), 1)
    placed = jnp.where(rows == lanes, numer, 0.0) + jnp.where(rows + K == lanes, denom, 0.0)
    line = jnp.sum(placed, axis=0, keepdims=True)
    s_ref[...] = jnp.broadcast_to(line[None], s_ref.shape)


def along(value, axis, step):
    n = lax.axis_size(axis)
    return lax.ppermute(value, axis, [(i, (i + step) % n) for i in range(n)])


def exchange(faces):
    right = along(faces[3], "col", 1)
    left = along(faces[2], "col", -1)
    return along(faces[1], "row", 1), along(faces[0], "row", -1), right, left


def shards(dual_ops, basis, coarse_inverse, gap_rhs, coarse_rhs, contact_mask):
    n_rows, n_cols = lax.axis_size("row"), lax.axis_size("col")
    row, col = lax.axis_index("row"), lax.axis_index("col")
    has_nb = jnp.stack([row > 0, row < n_rows - 1, col > 0, col < n_cols - 1]).astype(jnp.int32)
    dual = dual_ops[0, 0]

    vec = ((4, K, FACE), F32)
    face = ((K, FACE), F32)
    amps = ((K, 128), F32)
    half = ((2, K, FACE), F32)
    half_lhs = ((2 * K, M // 2), BF16)

    def gather(sent):
        return lax.all_to_all(sent, "row", 0, 0, tiled=True)

    def amplitudes(got):
        (parts,) = call(
            coarse_kernel, [((n_cols, K + K // 2, 128), F32)], got, *tile,
            scratch=[((2 * K, n_rows * MDEV), BF16)],
        )
        parts = lax.all_to_all(parts, "col", 0, 0, tiled=True)
        return call(amps_kernel, [amps, amps], parts)

    def sides(own):
        return along(own, "row", 1), along(own, "row", -1)

    def col_half(own, pair, grad):
        return call(
            col_half_kernel, [half, vec, face], has_nb, own, pair, grad, exp, dual,
            scratch=[half_lhs], smem=(0,), cost=8 << 20,
        )

    def first(*args):
        slabs = 16
        return pl.pallas_call(
            first_kernel,
            out_shape=[jax.ShapeDtypeStruct(*vec)] + [jax.ShapeDtypeStruct(*face)] * 4,
            in_specs=[pl.BlockSpec(memory_space=pltpu.VMEM)] * (len(args) - 1)
            + [pl.BlockSpec(memory_space=pltpu.HBM)],
            out_specs=[pl.BlockSpec(memory_space=pltpu.VMEM)] * 5,
            scratch_shapes=[
                pltpu.VMEM((slabs, M // slabs, M), F32),
                pltpu.VMEM((2 * K, M), BF16),
                pltpu.SemaphoreType.DMA((slabs,)),
            ],
            compiler_params=pltpu.CompilerParams(vmem_limit_bytes=VMEM_LIMIT),
        )(*args[:-1], pltpu.with_memory_space_constraint(args[-1], pltpu.HBM))

    rhs = coarse_rhs[0, 0]
    packed = jnp.concatenate([rhs[: K // 2], rhs[K // 2 :]], axis=1)
    got = gather(jnp.broadcast_to(packed[None], (n_rows, K // 2, 2 * MDEV)))
    tile = split_tile(coarse_inverse)
    mask = jnp.broadcast_to(contact_mask[0, 0, :, None, :].astype(F32), (4, 8, FACE))
    both = jnp.concatenate([basis[0, 0], gap_rhs[0, 0], mask], axis=1)
    both = [both[f] for f in range(4)]
    own, pair = amplitudes(got)

    nbs = exchange(both)
    exp, res, dvec, contact = call(
        weights_kernel,
        [((4, 256, FACE), BF16), ((M, 128), BF16), vec, ((4, FACE), jnp.int32)],
        has_nb, *both, *nbs,
        smem=(0,),
    )
    multipliers, *faces = first(own, pair, *sides(own), exp, dual)
    faces, res, dvec, contact = lax.optimization_barrier((faces, res, dvec, contact))
    nbs = exchange(faces)
    for step in range(ITERS):
        grad, sent = call(
            grad_kernel,
            [vec, ((n_rows, K // 2, 128), F32)],
            has_nb, *faces, *nbs, dvec, res,
            scratch=[((2 * K, M), BF16)], smem=(0,),
        )
        own, pair = amplitudes(gather(sent))
        projected, image, sums = call(
            image_kernel,
            [vec, vec, ((n_rows * n_cols, 1, 128), F32)],
            has_nb, own, *sides(own), grad, *col_half(own, pair, grad), exp, dual,
            scratch=[half_lhs], smem=(0,),
        )
        sums = lax.all_to_all(sums, ("row", "col"), 0, 0, tiled=True)
        if step + 1 < ITERS:
            ratio, corr, *sent_faces = call(
                step_kernel, [amps, vec] + [face] * 4,
                has_nb, sums, contact, multipliers, projected, image, *faces, dual,
                scratch=[((2 * K, FACE), BF16)], smem=(0,),
            )
            nbs = exchange(sent_faces)
            multipliers, *faces = call(
                outer_kernel, [vec] + [face] * 4,
                has_nb, ratio, contact, multipliers, projected, corr, *sent_faces, dual,
                scratch=[((2 * K, FACE), BF16)], smem=(0,), cost=4 << 20,
            )
        else:
            (multipliers,) = call(last_kernel, [vec], sums, contact, multipliers, projected)
    return (multipliers[None, None], projected[None, None])


def solution(mesh):
    return jax.shard_map(
        shards,
        mesh=mesh,
        in_specs=(
            P("row", "col", None, None),
            P("row", "col", None, None, None),
            P("row", "col"),
            P("row", "col", None, None, None),
            P("row", "col", None, None),
            P("row", "col", None, None),
        ),
        out_specs=(P("row", "col", None, None, None), P("row", "col", None, None, None)),
        check_vma=False,
    )
```
